512 devices in a mesh: seq: 64 (over z, y_hi, x), head: 8 (over y_lo, core).
Axes of the slice: x: 4, y: 8 (y_hi: 2, y_lo: 4; y = y_hi * 4 + y_lo), z: 8, core: 2. Of those that a mesh axis runs over, the one named last changes fastest.
Arguments:
- queries: bfloat16 [10240, 1024], P('seq', 'head'), may hold values from -15 to 15
- key_vectors: bfloat16 [10240, 1024], P('seq', 'head'), may hold values from -15 to 15
- value_vectors: bfloat16 [10240, 1024], P('seq', 'head'), may hold values from -6 to 6
- query_tangent: bfloat16 [10240, 1024], P('seq', 'head'), may hold values from -6 to 6
- key_tangent: bfloat16 [10240, 1024], P('seq', 'head'), may hold values from -6 to 6
- value_tangent: bfloat16 [10240, 1024], P('seq', 'head'), may hold values from -6 to 6
- out_weight: bfloat16 [1024, 6144], P('head'), may hold values from -0.25 to 0.25
Outputs:
- layer_out: bfloat16 [10240, 6144], P('seq', 'head')
- layer_tangent: bfloat16 [10240, 6144], P('seq', 'head')
The draws below stay inside these ranges and needn't reach their ends.
All inputs are finite; a program needn't handle non-finite values.
Results may differ from the reference program's by a relative error of at most 0.02.
Values may be sent and summed in bfloat16 or wider, within the bound.
No kernel may reach another device: no remote copies, remote signals or barrier semaphores. Data moves between devices by JAX's collectives and lax.ppermute only.
A program may use at most 64 MiB of HBM per device.

```python
import jax
import jax.numpy as jnp
from jax import lax

D = 6144
HD = 128
HEADS_DEV = 1
TOK_DEV = 160
HEADS = 8
TOKENS = 10240
N_SEQ = 64
N_HEAD = 8


def draw_queries(key, part):
    key = jax.random.fold_in(key, 1)
    base = jnp.clip(jax.random.normal(key, (TOKENS, HEADS * HD), jnp.float32), -4.0, 4.0)
    return base.astype(jnp.bfloat16)


def draw_key_vectors(key, part):
    key = jax.random.fold_in(key, 2)
    base = 2.8 * jnp.clip(jax.random.normal(key, (TOKENS, HEADS * HD), jnp.float32), -4.0, 4.0)
    return base.astype(jnp.bfloat16)


def raised(values, stream_key, source, target, blocks, factor):
    owner, partner = [(jnp.arange(values.shape[dim]) // (values.shape[dim] // blocks)).reshape([-1 if axis == dim else 1 for axis in range(values.ndim)]) for dim in (source, target)]
    chosen = jax.random.permutation(stream_key, blocks)[partner]
    strong = (owner == chosen) | (owner == (partner + blocks // 2) % blocks)
    return jnp.where(strong, factor * values, values)


def block_scale(key, dims, shards, smallest, top_value):
    factor_of, own = 1.0, jax.random.fold_in(key, 6)
    for dim, parts in shards:
        draws = jnp.exp(jax.random.uniform(jax.random.fold_in(own, dim), (parts,), jnp.float32, smallest / len(shards), top_value / len(shards)))
        factor_of = factor_of * jnp.repeat(draws, dims[dim] // parts).reshape([-1 if axis == dim else 1 for axis in range(len(dims))])
    return factor_of


def gaussian(key, dims, width, limit, cuts=(), kind=jnp.bfloat16):
    array = width * jax.random.normal(key, dims, jnp.float32)
    if cuts:
        array = array * block_scale(key, dims, cuts, -0.22, 0.18)
    return jnp.clip(array, -limit, limit).astype(kind)


def gaussian_with(rng, shape, deviation, limit, split, heavy, held_as=jnp.bfloat16):
    values = deviation * jax.random.normal(rng, shape, jnp.float32)
    if split:
        values = values * block_scale(rng, shape, split, -0.22, 0.18)
    return jnp.clip(raised(values, jax.random.fold_in(rng, 3), *heavy), -limit, limit).astype(held_as)


def setup_inputs(seed: int = 0) -> dict:
    splits = jax.random.split(jax.random.key(seed), 8)
    queries = draw_queries(jax.random.fold_in(splits[7], 71), 0)
    key_vectors = draw_key_vectors(jax.random.fold_in(splits[7], 71), 0)
    value_vectors = gaussian(splits[2], (TOKENS, HEADS * HD), 1.0, 6.0, ((0, 64), (1, 8)))
    query_tangent = gaussian(splits[3], (TOKENS, HEADS * HD), 1.0, 6.0, ((0, 64), (1, 8)))
    key_tangent = gaussian(splits[4], (TOKENS, HEADS * HD), 1.0, 6.0, ((0, 64), (1, 8)))
    value_tangent = gaussian(splits[5], (TOKENS, HEADS * HD), 1.0, 6.0, ((0, 64), (1, 8)))
    out_weight = gaussian_with(splits[6], (HEADS * HD, D), (HEADS * HD) ** -0.5, 0.25, ((0, 8),), (0, 1, 8, 2.0))
    return {"queries": queries, "key_vectors": key_vectors, "value_vectors": value_vectors, "query_tangent": query_tangent, "key_tangent": key_tangent, "value_tangent": value_tangent, "out_weight": out_weight}


def attend_block(query_block, qtan_block, key_head, value_head, ktan_head, vtan_head):
    score_scale = HD ** -0.5
    scores = jnp.dot(query_block, key_head.T, preferred_element_type=jnp.float32) * score_scale
    score_tangent = (jnp.dot(qtan_block, key_head.T, preferred_element_type=jnp.float32)
                     + jnp.dot(query_block, ktan_head.T, preferred_element_type=jnp.float32)) * score_scale
    row_max = jnp.max(scores, axis=1, keepdims=True)
    exp_weights = jnp.exp(scores - row_max)
    row_total = jnp.sum(exp_weights, axis=1, keepdims=True)
    weighted = exp_weights * score_tangent
    row_grad = jnp.sum(weighted, axis=1, keepdims=True)
    exp_low = exp_weights.astype(jnp.bfloat16)
    weighted_low = weighted.astype(jnp.bfloat16)
    primal_acc = jnp.dot(exp_low, value_head, preferred_element_type=jnp.float32)
    tangent_acc = (jnp.dot(weighted_low, value_head, preferred_element_type=jnp.float32)
                   + jnp.dot(exp_low, vtan_head, preferred_element_type=jnp.float32))
    attn_out = primal_acc / row_total
    attn_tangent = tangent_acc / row_total - (row_grad / row_total) * attn_out
    return attn_out.astype(jnp.bfloat16), attn_tangent.astype(jnp.bfloat16)


def reference(queries, key_vectors, value_vectors, query_tangent, key_tangent, value_tangent, out_weight):
    def one_head(h):
        col_start = (h * HD).astype(jnp.int32)

        def slice_head(source):
            return lax.dynamic_slice_in_dim(source, col_start, HD, 1)

        query_head = slice_head(queries)
        qtan_head = slice_head(query_tangent)
        key_head = slice_head(key_vectors)
        value_head = slice_head(value_vectors)
        ktan_head = slice_head(key_tangent)
        vtan_head = slice_head(value_tangent)

        def one_block(b):
            row_start = (b * TOK_DEV).astype(jnp.int32)
            query_block = lax.dynamic_slice_in_dim(query_head, row_start, TOK_DEV, 0)
            qtan_block = lax.dynamic_slice_in_dim(qtan_head, row_start, TOK_DEV, 0)
            return attend_block(query_block, qtan_block, key_head, value_head, ktan_head, vtan_head)

        block_out, block_tan = lax.map(one_block, jnp.arange(N_SEQ, dtype=jnp.int32))
        return block_out.reshape(TOKENS, HD), block_tan.reshape(TOKENS, HD)

    head_outs, head_tans = lax.map(one_head, jnp.arange(HEADS, dtype=jnp.int32))
    layer_sum = jnp.zeros((TOKENS, D), jnp.float32)
    tangent_sum = jnp.zeros((TOKENS, D), jnp.float32)
    for head_group in range(N_HEAD):
        first_head = head_group * HEADS_DEV
        group_out = jnp.transpose(head_outs[first_head:first_head + HEADS_DEV], (1, 0, 2)).reshape(TOKENS, HEADS_DEV * HD)
        group_tan = jnp.transpose(head_tans[first_head:first_head + HEADS_DEV], (1, 0, 2)).reshape(TOKENS, HEADS_DEV * HD)
        group_weight = out_weight[first_head * HD:(first_head + HEADS_DEV) * HD]
        out_part = jnp.dot(group_out, group_weight, preferred_element_type=jnp.float32).astype(jnp.bfloat16)
        tangent_part = jnp.dot(group_tan, group_weight, preferred_element_type=jnp.float32).astype(jnp.bfloat16)
        out_part, tangent_part = lax.optimization_barrier((out_part, tangent_part))
        layer_sum = layer_sum + out_part.astype(jnp.float32)
        tangent_sum = tangent_sum + tangent_part.astype(jnp.float32)
    return layer_sum.astype(jnp.bfloat16), tangent_sum.astype(jnp.bfloat16)
```

```python
import jax, jax.numpy as jnp
from jax import lax
from jax.sharding import PartitionSpec as P
from jax.experimental import pallas as pl
from jax.experimental.pallas import tpu as pltpu

HD = 128
SCALE = HD ** -0.5
LOG2E = 1.4426950408889634
STAT = 16
F32 = jnp.float32
BF16 = jnp.bfloat16


def dot_nt(a, b):
    return lax.dot_general(a, b, (((1,), (1,)), ((), ())), preferred_element_type=F32)


def dot_nn(a, b):
    return jnp.dot(a, b, preferred_element_type=F32)


def three_parts(value):
    high = value.astype(BF16).astype(F32)
    rest = value - high
    mid = rest.astype(BF16).astype(F32)
    return high, mid, (rest - mid)


def attention_body(nq, nk, rows, step_blocks, place_ref, *refs):
    q_refs, k_refs = refs[:nq], refs[nq:nq + nk]
    out_ref, qq, kk, vv = refs[nq + nk:]
    at = 0
    for ref in q_refs:
        for b in range(ref.shape[0]):
            span = pl.ds(at * rows, rows)
            qq[span, :HD] = ref[b, rows:]
            qq[span, HD:] = ref[b, :rows]
            at += 1
    blocks = at
    at = 0
    for ref in k_refs:
        for b in range(ref.shape[0]):
            span = pl.ds(at * rows, rows)
            kk[span, :HD] = ref[b, :rows]
            vv[span, :HD] = ref[b, rows:2 * rows]
            kk[span, HD:] = ref[b, 2 * rows:3 * rows]
            vv[span, HD:] = ref[b, 3 * rows:]
            at += 1
    span_rows = step_blocks * rows
    lane = lax.broadcasted_iota(jnp.int32, (rows, HD), 1)
    pick_row = lax.broadcasted_iota(jnp.int32, (STAT, HD), 0)
    pick_lane = lax.broadcasted_iota(jnp.int32, (STAT, HD), 1)
    pick_low = (pick_row == pick_lane).astype(F32).astype(BF16)
    pick_high = (pick_row == pick_lane + STAT // 2).astype(F32)
    pick_high = jnp.where(pick_lane < STAT // 2, pick_high, 0.0).astype(BF16)
    pick_low = jnp.where(pick_row < STAT // 2, pick_low.astype(F32), 0.0).astype(BF16)

    def step(i, carry):
        span = pl.ds(pl.multiple_of(i * span_rows, span_rows), span_rows)
        scores = dot_nt(qq[span, HD:], kk[:, :HD])
        slope = dot_nt(qq[span, :], kk[...])
        top = jnp.max(scores, axis=1, keepdims=True)
        weights = jnp.exp2((scores - top) * (SCALE * LOG2E))
        total = jnp.sum(weights, axis=1, keepdims=True)
        sloped = weights * slope
        grad = jnp.sum(sloped, axis=1, keepdims=True)
        both = dot_nn(weights.astype(BF16), vv[...])
        extra = dot_nn(sloped.astype(BF16), vv[:, :HD])
        inverse = 1.0 / total
        mean = both[:, :HD] * inverse
        slope_mean = grad * (SCALE * inverse)
        tangent = (extra * SCALE + both[:, HD:]) * inverse - slope_mean * mean
        weight_log = top * SCALE + jnp.log(total)
        stats = three_parts(weight_log) + three_parts(slope_mean)
        for b in range(step_blocks):
            part = slice(b * rows, (b + 1) * rows)
            at = place_ref[i * step_blocks + b]
            out_ref[at, :rows, :] = mean[part].astype(BF16)
            out_ref[at, rows:2 * rows, :] = tangent[part].astype(BF16)
            table = jnp.zeros((rows, HD), F32)
            for n, stat in enumerate(stats):
                table = jnp.where(lane == n, stat[part], table)
            table = jnp.concatenate([table, jnp.zeros((2 * HD - rows, HD), F32)]).astype(BF16)
            turned = dot_nt(pick_low, table[:HD]) + dot_nt(pick_high, table[HD:])
            out_ref[at, 2 * rows:, :] = turned.astype(BF16)
        return carry

    lax.fori_loop(0, blocks // step_blocks, step, 0, unroll=False)


def attention(places, q_parts, k_parts, rows, step_blocks=2):
    nblocks = sum(p.shape[0] for p in q_parts)
    nkeys = sum(p.shape[0] for p in k_parts) * rows
    body = lambda *refs: attention_body(len(q_parts), len(k_parts), rows, step_blocks, *refs)
    whole = pl.BlockSpec(memory_space=pltpu.VMEM)
    work = nblocks * rows * nkeys * HD
    return pl.pallas_call(
        body,
        out_shape=jax.ShapeDtypeStruct((nblocks, 2 * rows + STAT, HD), BF16),
        in_specs=[pl.BlockSpec(memory_space=pltpu.SMEM)] + [whole] * (len(q_parts) + len(k_parts)),
        out_specs=whole,
        scratch_shapes=[
            pltpu.VMEM((nblocks * rows, 2 * HD), BF16),
            pltpu.VMEM((nkeys, 2 * HD), BF16),
            pltpu.VMEM((nkeys, 2 * HD), BF16),
        ],
        compiler_params=pltpu.CompilerParams(vmem_limit_bytes=48 * 1024 * 1024),
        cost_estimate=pl.CostEstimate(flops=12 * work, bytes_accessed=4000000, transcendentals=work // HD),
        name="attention",
    )(places, *q_parts, *k_parts)


def merge_body(count, rows, part_ref, out_ref):
    pick_row = lax.broadcasted_iota(jnp.int32, (STAT, HD), 0)

    def pick(first, last):
        return jnp.where((pick_row >= first) & (pick_row < last), 1.0, 0.0).astype(BF16)

    def column(block, first):
        turned = lambda p: lax.dot_general(block, p, (((0,), (0,)), ((), ())), preferred_element_type=F32)
        low = turned(pick(first, first + 3))
        high = turned(pick(first + 8, first + 11))
        return jnp.concatenate([low, high[:rows - HD]])

    logs, slopes = [], []
    for b in range(count):
        block = part_ref[b, 2 * rows:, :]
        logs.append(column(block, 0))
        slopes.append(column(block, 3))
    top = logs[0]
    for b in range(1, count):
        top = jnp.maximum(top, logs[b])
    shares = [jnp.exp(one - top) for one in logs]
    total = sum(shares[1:], shares[0])
    inverse = 1.0 / total
    shares = [one * inverse for one in shares]
    slope_mean = shares[0] * slopes[0]
    for b in range(1, count):
        slope_mean += shares[b] * slopes[b]
    mean = jnp.zeros((rows, HD), F32)
    tangent = jnp.zeros((rows, HD), F32)
    for b in range(count):
        one = part_ref[b, :rows, :].astype(F32)
        mean += shares[b] * one
        tangent += shares[b] * (part_ref[b, rows:2 * rows, :].astype(F32) + (slopes[b] - slope_mean) * one)
    out_ref[:rows, :] = mean.astype(BF16)
    out_ref[rows:, :] = tangent.astype(BF16)


def merge(parts, rows):
    whole = pl.BlockSpec(memory_space=pltpu.VMEM)
    return pl.pallas_call(
        lambda *refs: merge_body(parts.shape[0], rows, *refs),
        out_shape=jax.ShapeDtypeStruct((2 * rows, HD), BF16),
        in_specs=[whole],
        out_specs=whole,
        compiler_params=pltpu.CompilerParams(vmem_limit_bytes=32 * 1024 * 1024),
        name="merge",
    )(parts)


def project_body(count, columns, core_ref, *refs):
    attn, weight = refs[:count], refs[count:2 * count]
    keep_ref, give_ref, left, right = refs[2 * count:]
    for n in range(count):
        left[:, n * HD:(n + 1) * HD] = attn[n][...]
        right[n * HD:(n + 1) * HD, :] = weight[n][...]
    core = core_ref[0]
    mine = pl.ds(pl.multiple_of(core * columns, HD), columns)
    other = pl.ds(pl.multiple_of((1 - core) * columns, HD), columns)
    give_ref[...] = dot_nn(left[...], right[:, other]).astype(BF16)
    keep_ref[...] = dot_nn(left[...], right[:, mine])


def project(core, attn, weight):
    rows, columns = attn[0].shape[0], weight[0].shape[1] // 2
    count = len(attn)
    whole = pl.BlockSpec(memory_space=pltpu.VMEM)
    return pl.pallas_call(
        lambda *refs: project_body(count, columns, *refs),
        out_shape=(
            jax.ShapeDtypeStruct((rows, columns), F32),
            jax.ShapeDtypeStruct((rows, columns), BF16),
        ),
        in_specs=[pl.BlockSpec(memory_space=pltpu.SMEM)] + [whole] * (2 * count),
        out_specs=(whole, whole),
        scratch_shapes=[
            pltpu.VMEM((rows, count * HD), BF16),
            pltpu.VMEM((count * HD, 2 * columns), BF16),
        ],
        compiler_params=pltpu.CompilerParams(vmem_limit_bytes=32 * 1024 * 1024),
        cost_estimate=pl.CostEstimate(flops=4 * rows * count * HD * columns, bytes_accessed=4000000, transcendentals=0),
        name="project",
    )(core, *attn, *weight)


def add_body(rows, keep_ref, got_ref, out_ref, tan_ref):
    out_ref[...] = (keep_ref[:rows] + got_ref[:rows].astype(F32)).astype(BF16)
    tan_ref[...] = (keep_ref[rows:] + got_ref[rows:].astype(F32)).astype(BF16)


def add_halves(keep, got):
    rows, columns = keep.shape[0] // 2, keep.shape[1]
    whole = pl.BlockSpec(memory_space=pltpu.VMEM)
    one = jax.ShapeDtypeStruct((rows, columns), BF16)
    return pl.pallas_call(
        lambda *refs: add_body(rows, *refs),
        out_shape=(one, one),
        in_specs=[whole, whole],
        out_specs=(whole, whole),
        name="add_halves",
    )(keep, got)


def turn(array, axis, count, offset):
    return lax.ppermute(array, axis, [(i, (i + offset) % count) for i in range(count)])


def per_device(queries, key_vectors, value_vectors, query_tangent, key_tangent, value_tangent, out_weight):
    rows = queries.shape[0]
    yh, x, yl, core = (lax.axis_index(name) for name in ("yh", "x", "yl", "c"))
    columns = out_weight.shape[1] // 4

    q_own = jnp.concatenate([queries, query_tangent])
    q_far = turn(q_own, "yh", 2, 1)
    k_own = jnp.concatenate([key_vectors, value_vectors, key_tangent, value_tangent])
    k_near = lax.all_gather(k_own, "zh", axis=0)
    k_pair = turn(k_near, "zl", 2, 1)
    q_pair = jnp.stack([q_own, q_far])
    q_parts = [q_pair] + [turn(q_pair, "x", 4, n) for n in (1, 2, 3)]
    w_parts = [lax.dynamic_slice_in_dim(out_weight, ((yl + n) % 4) * columns, columns, 1) for n in range(4)]
    w_parts = [w_parts[0]] + [turn(w_parts[n], "yl", 4, n) for n in (1, 2, 3)]

    row = jnp.arange(8, dtype=jnp.int32)
    places = ((x - row // 2) % 4) * 2 + jnp.where(row % 2 == 0, yh, 1 - yh)
    partial = attention(places.astype(jnp.int32), q_parts, [k_near, k_pair], rows)
    parts = lax.all_to_all(partial, ("x", "yh"), 0, 0, tiled=True)
    attn = merge(parts, rows)
    a_parts = [attn] + [turn(attn, "yl", 4, n) for n in (1, 2, 3)]
    keep, give = project(core.astype(jnp.int32).reshape(1), a_parts, w_parts)
    got = turn(give, "c", 2, 1)
    return add_halves(keep, got)


def solution(mesh):
    split = jax.sharding.Mesh(
        mesh.devices.reshape(4, 2, 2, 4, 4, 2), ("zh", "zl", "yh", "x", "yl", "c")
    )
    seq, head = ("zh", "zl", "yh", "x"), ("yl", "c")
    block = P(seq, head)
    return jax.shard_map(
        per_device,
        mesh=split,
        in_specs=(block,) * 6 + (P(head, None),),
        out_specs=(block, block),
        check_vma=False,
    )
```

```python
import jax, jax.numpy as jnp
from jax import lax
from jax.sharding import PartitionSpec as P
from jax.experimental import pallas as pl
from jax.experimental.pallas import tpu as pltpu

HD = 128
SCALE = HD ** -0.5
LOG2E = 1.4426950408889634
STAT = 16
F32 = jnp.float32
BF16 = jnp.bfloat16


def dot_nt(a, b):
    return lax.dot_general(a, b, (((1,), (1,)), ((), ())), preferred_element_type=F32)


def dot_nn(a, b):
    return jnp.dot(a, b, preferred_element_type=F32)


def three_parts(value):
    high = value.astype(BF16).astype(F32)
    rest = value - high
    mid = rest.astype(BF16).astype(F32)
    return high, mid, (rest - mid)


WHOLE = pl.BlockSpec(memory_space=pltpu.VMEM)
SCALAR = pl.BlockSpec(memory_space=pltpu.SMEM)


def limit(mib):
    return pltpu.CompilerParams(vmem_limit_bytes=mib * 1024 * 1024)


def stat_rows(stats, rows):
    lane = lax.broadcasted_iota(jnp.int32, (rows, HD), 1)
    pick_row = lax.broadcasted_iota(jnp.int32, (STAT, HD), 0)
    pick_lane = lax.broadcasted_iota(jnp.int32, (STAT, HD), 1)
    half = STAT // 2
    low = jnp.where((pick_row == pick_lane) & (pick_row < half), 1.0, 0.0).astype(BF16)
    high = jnp.where((pick_row == pick_lane + half) & (pick_lane < half), 1.0, 0.0).astype(BF16)
    table = jnp.zeros((rows, HD), F32)
    for n, stat in enumerate(stats):
        table = jnp.where(lane == n, stat, table)
    table = jnp.concatenate([table, jnp.zeros((2 * HD - rows, HD), F32)]).astype(BF16)
    return (dot_nt(low, table[:HD]) + dot_nt(high, table[HD:])).astype(BF16)


def stat_columns(block, rows, first):
    pick_row = lax.broadcasted_iota(jnp.int32, (STAT, HD), 0)

    def turned(at):
        pick = jnp.where((pick_row >= at) & (pick_row < at + 3), 1.0, 0.0).astype(BF16)
        return lax.dot_general(block, pick, (((0,), (0,)), ((), ())), preferred_element_type=F32)

    return jnp.concatenate([turned(first), turned(first + STAT // 2)[: rows - HD]])


def attention_tile(q_ref, kk, vv, span):
    scores = dot_nt(q_ref[span, HD:], kk[:, :HD])
    slope = dot_nt(q_ref[span, :], kk[...])
    top = jnp.max(scores, axis=1, keepdims=True)
    weights = jnp.exp2((scores - top) * (SCALE * LOG2E))
    total = jnp.sum(weights, axis=1, keepdims=True)
    sloped = weights * slope
    grad = jnp.sum(sloped, axis=1, keepdims=True)
    both = dot_nn(weights.astype(BF16), vv[...])
    extra = dot_nn(sloped.astype(BF16), vv[:, :HD])
    inverse = 1.0 / total
    mean = both[:, :HD] * inverse
    slope_mean = grad * (SCALE * inverse)
    tangent = (extra * SCALE + both[:, HD:]) * inverse - slope_mean * mean
    return mean, tangent, top * SCALE + jnp.log(total), slope_mean


def attention_body(rows, step_blocks, place_ref, qa_ref, qb_ref, ka_ref, kb_ref, out_ref, qq, kk, vv):
    at = 0
    for q_ref in (qa_ref, qb_ref):
        for b in range(q_ref.shape[0]):
            span = pl.ds(at * rows, rows)
            qq[span, :HD] = q_ref[b, rows:]
            qq[span, HD:] = q_ref[b, :rows]
            at += 1
    blocks, at = at, 0
    for k_ref in (ka_ref, kb_ref):
        for b in range(k_ref.shape[0]):
            span = pl.ds(at * rows, rows)
            kk[span, :HD] = k_ref[b, :rows]
            vv[span, :HD] = k_ref[b, rows:2 * rows]
            kk[span, HD:] = k_ref[b, 2 * rows:3 * rows]
            vv[span, HD:] = k_ref[b, 3 * rows:]
            at += 1
    span_rows = step_blocks * rows

    def step(i, carry):
        span = pl.ds(pl.multiple_of(i * span_rows, span_rows), span_rows)
        mean, tangent, log, slope = attention_tile(qq, kk, vv, span)
        stats = three_parts(log) + three_parts(slope)
        for b in range(step_blocks):
            part = slice(b * rows, (b + 1) * rows)
            at = place_ref[i * step_blocks + b]
            out_ref[at, :rows, :] = mean[part].astype(BF16)
            out_ref[at, rows:2 * rows, :] = tangent[part].astype(BF16)
            out_ref[at, 2 * rows:, :] = stat_rows([s[part] for s in stats], rows)
        return carry

    lax.fori_loop(0, blocks // step_blocks, step, 0)


def attention(places, queries, keys, rows, step_blocks=4):
    blocks, nkeys = (sum(p.shape[0] for p in parts) for parts in (queries, keys))
    nkeys *= rows
    work = blocks * rows * nkeys * HD
    return pl.pallas_call(
        lambda *refs: attention_body(rows, step_blocks, *refs),
        out_shape=jax.ShapeDtypeStruct((blocks, 2 * rows + STAT, HD), BF16),
        in_specs=[SCALAR] + [WHOLE] * 4,
        out_specs=WHOLE,
        scratch_shapes=[
            pltpu.VMEM((blocks * rows, 2 * HD), BF16),
            pltpu.VMEM((nkeys, 2 * HD), BF16),
            pltpu.VMEM((nkeys, 2 * HD), BF16),
        ],
        compiler_params=limit(32),
        cost_estimate=pl.CostEstimate(flops=12 * work, bytes_accessed=4000000, transcendentals=work // HD),
        name="attention",
    )(places, *queries, *keys)


def merged(blocks, rows):
    logs = [stat_columns(block[2 * rows:, :], rows, 0) for block in blocks]
    slopes = [stat_columns(block[2 * rows:, :], rows, 3) for block in blocks]
    top = logs[0]
    for log in logs[1:]:
        top = jnp.maximum(top, log)
    shares = [jnp.exp(log - top) for log in logs]
    total = sum(shares[1:], shares[0])
    inverse = 1.0 / total
    slope_mean = sum([s * g for s, g in zip(shares[1:], slopes[1:])], shares[0] * slopes[0]) * inverse
    mean = jnp.zeros((rows, HD), F32)
    tangent = jnp.zeros((rows, HD), F32)
    for block, share, slope in zip(blocks, shares, slopes):
        one = block[:rows, :].astype(F32)
        mean += share * one
        tangent += share * (block[rows:2 * rows, :].astype(F32) + (slope - slope_mean) * one)
    return mean * inverse, tangent * inverse, top + jnp.log(total), slope_mean


def merge_body(rows, copies, part_ref, out_ref):
    mean, tangent, _, _ = merged([part_ref[b] for b in range(part_ref.shape[0])], rows)
    for n in range(copies):
        out_ref[n, :rows, :] = mean.astype(BF16)
        out_ref[n, rows:, :] = tangent.astype(BF16)


def merge(parts, rows, copies):
    return pl.pallas_call(
        lambda *refs: merge_body(rows, copies, *refs),
        out_shape=jax.ShapeDtypeStruct((copies, 2 * rows, HD), BF16),
        in_specs=[WHOLE],
        out_specs=WHOLE,
        compiler_params=limit(12),
        name="merge",
    )(parts)


def project_body(count, columns, at_ref, attn_ref, own_ref, *refs):
    here, there = refs[:count - 1], refs[count - 1]
    keep_ref, give_ref, left, right = refs[count:]
    core, half, part = at_ref[0], at_ref[1], HD // 2
    right[:HD, :] = own_ref[...]
    for n in range(count):
        left[:, n * HD:(n + 1) * HD] = attn_ref[at_ref[2 + n]]
        if n:
            right[pl.ds(pl.multiple_of(n * HD + half * part, part), part), :] = here[n - 1][...]
            right[pl.ds(pl.multiple_of(n * HD + (1 - half) * part, part), part), :] = there[n - 1]
    mine = pl.ds(pl.multiple_of(core * columns, HD), columns)
    other = pl.ds(pl.multiple_of((1 - core) * columns, HD), columns)
    give_ref[...] = dot_nn(left[...], right[:, other]).astype(BF16)
    keep_ref[...] = dot_nn(left[...], right[:, mine])


def project(places, attn, own, here, there):
    rows, columns, count = attn.shape[1], own.shape[1] // 2, attn.shape[0]
    return pl.pallas_call(
        lambda *refs: project_body(count, columns, *refs),
        out_shape=(
            jax.ShapeDtypeStruct((rows, columns), F32),
            jax.ShapeDtypeStruct((rows, columns), BF16),
        ),
        in_specs=[SCALAR] + [WHOLE] * (2 + count),
        out_specs=(WHOLE, WHOLE),
        scratch_shapes=[
            pltpu.VMEM((rows, count * HD), BF16),
            pltpu.VMEM((count * HD, 2 * columns), BF16),
        ],
        compiler_params=limit(12),
        cost_estimate=pl.CostEstimate(flops=4 * rows * count * HD * columns, bytes_accessed=4000000, transcendentals=0),
        name="project",
    )(places, attn, own, *here, there)


def add_body(rows, keep_ref, got_ref, out_ref, tan_ref):
    out_ref[...] = (keep_ref[:rows] + got_ref[:rows].astype(F32)).astype(BF16)
    tan_ref[...] = (keep_ref[rows:] + got_ref[rows:].astype(F32)).astype(BF16)


def add_halves(keep, got):
    rows, columns = keep.shape[0] // 2, keep.shape[1]
    one = jax.ShapeDtypeStruct((rows, columns), BF16)
    return pl.pallas_call(
        lambda *refs: add_body(rows, *refs),
        out_shape=(one, one),
        in_specs=[WHOLE, WHOLE],
        out_specs=(WHOLE, WHOLE),
        compiler_params=limit(4),
        name="add_halves",
    )(keep, got)


def prepare_body(rows, copies, q_ref, k_ref, v_ref, qt_ref, kt_ref, vt_ref, queries_ref, keys_ref, spread_ref):
    queries_ref[:rows, :] = q_ref[...]
    queries_ref[rows:, :] = qt_ref[...]
    for n, ref in enumerate((k_ref, v_ref, kt_ref, vt_ref)):
        span = pl.ds(n * rows, rows)
        value = ref[...]
        keys_ref[span, :] = value
        for m in range(copies):
            spread_ref[m, span, :] = value


def prepare(arrays, copies):
    rows = arrays[0].shape[0]
    return pl.pallas_call(
        lambda *refs: prepare_body(rows, copies, *refs),
        out_shape=(
            jax.ShapeDtypeStruct((2 * rows, HD), BF16),
            jax.ShapeDtypeStruct((4 * rows, HD), BF16),
            jax.ShapeDtypeStruct((copies, 4 * rows, HD), BF16),
        ),
        grid=(1,),
        in_specs=[pl.BlockSpec((rows, HD), lambda i: (0, 0))] * 6,
        out_specs=(WHOLE,) * 3,
        compiler_params=limit(56),
        name="prepare",
    )(*arrays)


def turn(array, axis, count, offset):
    return lax.ppermute(array, axis, [(i, (i + offset) % count) for i in range(count)])


def spread(array, axis, count):
    return lax.all_to_all(jnp.broadcast_to(array[None], (count,) + array.shape), axis, 0, 0, tiled=True)


def per_device(queries, key_vectors, value_vectors, query_tangent, key_tangent, value_tangent, out_weight):
    rows = queries.shape[0]
    yl, zl, core = lax.axis_index("yl"), lax.axis_index("zl"), lax.axis_index("c")
    columns = out_weight.shape[1] // 4

    arrays = (queries, key_vectors, value_vectors, query_tangent, key_tangent, value_tangent)
    q_own, k_own, k_spread = prepare(arrays, 4)
    k_first = lax.all_to_all(k_spread, "zh", 0, 0, tiled=True)
    k_far = turn(k_own, "yh", 2, 1)
    q_near = lax.all_gather(q_own, "x", axis=0)
    q_near, k_first, k_far = lax.optimization_barrier((q_near, k_first, k_far))
    k_second = spread(k_far, "zh", 4)
    q_pair = turn(q_near, "zl", 2, 1)

    def weight_of(n, first, height):
        at = (first, ((yl + n) % 4) * columns)
        return lax.dynamic_slice(out_weight, at, (height, columns))

    w_own = weight_of(0, 0, HD)
    w_here = [turn(weight_of(n, zl * (HD // 2), HD // 2), "yl", 4, n) for n in (1, 2, 3)]

    block = jnp.arange(8)
    spots = ((block % 4) * 2 + jnp.where(block < 4, zl, 1 - zl)).astype(jnp.int32)
    partial = attention(spots, (q_near, q_pair), (k_first, k_second), rows)
    partial, w_here = lax.optimization_barrier((partial, w_here))
    parts = lax.all_to_all(partial, ("x", "zl"), 0, 0, tiled=True)
    near = [(z, (z + 1) % 8 if z % 2 else (z - 1) % 8) for z in range(8)]
    w_there = lax.ppermute(jnp.stack(w_here), ("zh", "zl"), near)
    attn = lax.all_to_all(merge(parts, rows, 4), "yl", 0, 0, tiled=True)
    places = jnp.stack([core, zl] + [(yl - n) % 4 for n in range(4)]).astype(jnp.int32)
    keep, give = project(places, attn, w_own, w_here, w_there)
    got = turn(give, "c", 2, 1)
    return add_halves(keep, got)


def solution(mesh):
    split = jax.sharding.Mesh(
        mesh.devices.reshape(4, 2, 2, 4, 4, 2), ("zh", "zl", "yh", "x", "yl", "c")
    )
    seq, head = ("zh", "zl", "yh", "x"), ("yl", "c")
    block = P(seq, head)
    return jax.shard_map(
        per_device,
        mesh=split,
        in_specs=(block,) * 6 + (P(head, None),),
        out_specs=(block, block),
        check_vma=False,
    )
```

```python
import jax, jax.numpy as jnp
from jax import lax
from jax.sharding import PartitionSpec as P
from jax.experimental import pallas as pl
from jax.experimental.pallas import tpu as pltpu

HD = 128
SCALE = HD ** -0.5
LOG2E = 1.4426950408889634
STAT = 16
F32 = jnp.float32
BF16 = jnp.bfloat16


def dot_nt(a, b):
    return lax.dot_general(a, b, (((1,), (1,)), ((), ())), preferred_element_type=F32)


def dot_nn(a, b):
    return jnp.dot(a, b, preferred_element_type=F32)


def three_parts(value):
    high = value.astype(BF16).astype(F32)
    rest = value - high
    mid = rest.astype(BF16).astype(F32)
    return high, mid, (rest - mid)


WHOLE = pl.BlockSpec(memory_space=pltpu.VMEM)
SCALAR = pl.BlockSpec(memory_space=pltpu.SMEM)


def limit(mib):
    return pltpu.CompilerParams(vmem_limit_bytes=mib * 1024 * 1024)


def stat_rows(stats, rows):
    lane = lax.broadcasted_iota(jnp.int32, (rows, HD), 1)
    pick_row = lax.broadcasted_iota(jnp.int32, (STAT, HD), 0)
    pick_lane = lax.broadcasted_iota(jnp.int32, (STAT, HD), 1)
    half = STAT // 2
    low = jnp.where((pick_row == pick_lane) & (pick_row < half), 1.0, 0.0).astype(BF16)
    high = jnp.where((pick_row == pick_lane + half) & (pick_lane < half), 1.0, 0.0).astype(BF16)
    table = jnp.zeros((rows, HD), F32)
    for n, stat in enumerate(stats):
        table = jnp.where(lane == n, stat, table)
    table = jnp.concatenate([table, jnp.zeros((2 * HD - rows, HD), F32)]).astype(BF16)
    return (dot_nt(low, table[:HD]) + dot_nt(high, table[HD:])).astype(BF16)


def stat_columns(block, rows, first):
    pick_row = lax.broadcasted_iota(jnp.int32, (STAT, HD), 0)

    def turned(at):
        pick = jnp.where((pick_row >= at) & (pick_row < at + 3), 1.0, 0.0).astype(BF16)
        return lax.dot_general(block, pick, (((0,), (0,)), ((), ())), preferred_element_type=F32)

    return jnp.concatenate([turned(first), turned(first + STAT // 2)[: rows - HD]])


def attention_tile(q_ref, kk, vv, span):
    scores = dot_nt(q_ref[span, HD:], kk[:, :HD])
    slope = dot_nt(q_ref[span, :], kk[...])
    top = jnp.max(scores, axis=1, keepdims=True)
    weights = jnp.exp2((scores - top) * (SCALE * LOG2E))
    total = jnp.sum(weights, axis=1, keepdims=True)
    sloped = weights * slope
    grad = jnp.sum(sloped, axis=1, keepdims=True)
    both = dot_nn(weights.astype(BF16), vv[...])
    extra = dot_nn(sloped.astype(BF16), vv[:, :HD])
    inverse = 1.0 / total
    mean = both[:, :HD] * inverse
    slope_mean = grad * (SCALE * inverse)
    tangent = (extra * SCALE + both[:, HD:]) * inverse - slope_mean * mean
    return mean, tangent, top * SCALE + jnp.log(total), slope_mean


def attention_body(rows, step_blocks, q_ref, ka_ref, kb_ref, out_ref, qq, kk, vv):
    blocks = q_ref.shape[0]
    for b in range(blocks):
        span = pl.ds(b * rows, rows)
        qq[span, :HD] = q_ref[b, rows:]
        qq[span, HD:] = q_ref[b, :rows]
    for n, k_ref in enumerate((ka_ref, kb_ref)):
        for b in range(k_ref.shape[0]):
            span = pl.ds((n * k_ref.shape[0] + b) * rows, rows)
            kk[span, :HD] = k_ref[b, :rows]
            vv[span, :HD] = k_ref[b, rows:2 * rows]
            kk[span, HD:] = k_ref[b, 2 * rows:3 * rows]
            vv[span, HD:] = k_ref[b, 3 * rows:]
    span_rows = step_blocks * rows

    def step(i, carry):
        span = pl.ds(pl.multiple_of(i * span_rows, span_rows), span_rows)
        mean, tangent, log, slope = attention_tile(qq, kk, vv, span)
        stats = three_parts(log) + three_parts(slope)
        for b in range(step_blocks):
            part = slice(b * rows, (b + 1) * rows)
            at = i * step_blocks + b
            out_ref[at, :rows, :] = mean[part].astype(BF16)
            out_ref[at, rows:2 * rows, :] = tangent[part].astype(BF16)
            out_ref[at, 2 * rows:, :] = stat_rows([s[part] for s in stats], rows)
        return carry

    lax.fori_loop(0, blocks // step_blocks, step, 0)


def attention(queries, keys, rows, step_blocks=4):
    blocks, nkeys = queries.shape[0], sum(p.shape[0] for p in keys) * rows
    work = blocks * rows * nkeys * HD
    return pl.pallas_call(
        lambda *refs: attention_body(rows, step_blocks, *refs),
        out_shape=jax.ShapeDtypeStruct((blocks, 2 * rows + STAT, HD), BF16),
        in_specs=[WHOLE] * 3,
        out_specs=WHOLE,
        scratch_shapes=[
            pltpu.VMEM((blocks * rows, 2 * HD), BF16),
            pltpu.VMEM((nkeys, 2 * HD), BF16),
            pltpu.VMEM((nkeys, 2 * HD), BF16),
        ],
        compiler_params=limit(32),
        cost_estimate=pl.CostEstimate(flops=12 * work, bytes_accessed=4000000, transcendentals=work // HD),
        name="attention",
    )(queries, *keys)


def merged(blocks, rows):
    logs = [stat_columns(block[2 * rows:, :], rows, 0) for block in blocks]
    slopes = [stat_columns(block[2 * rows:, :], rows, 3) for block in blocks]
    top = logs[0]
    for log in logs[1:]:
        top = jnp.maximum(top, log)
    shares = [jnp.exp(log - top) for log in logs]
    total = sum(shares[1:], shares[0])
    inverse = 1.0 / total
    slope_mean = sum([s * g for s, g in zip(shares[1:], slopes[1:])], shares[0] * slopes[0]) * inverse
    mean = jnp.zeros((rows, HD), F32)
    tangent = jnp.zeros((rows, HD), F32)
    for block, share, slope in zip(blocks, shares, slopes):
        one = block[:rows, :].astype(F32)
        mean += share * one
        tangent += share * (block[rows:2 * rows, :].astype(F32) + (slope - slope_mean) * one)
    return mean * inverse, tangent * inverse, top + jnp.log(total), slope_mean


def merge_body(rows, part_ref, out_ref):
    mean, tangent, _, _ = merged([part_ref[b] for b in range(part_ref.shape[0])], rows)
    out_ref[:rows, :] = mean.astype(BF16)
    out_ref[rows:, :] = tangent.astype(BF16)


def merge(parts, rows):
    return pl.pallas_call(
        lambda *refs: merge_body(rows, *refs),
        out_shape=jax.ShapeDtypeStruct((2 * rows, HD), BF16),
        in_specs=[WHOLE],
        out_specs=WHOLE,
        compiler_params=limit(12),
        name="merge",
    )(parts)


def cut_body(columns, at_ref, own_ref, next_ref, half_ref, keep_ref, give_ref):
    core = at_ref[0]
    mine = pl.ds(pl.multiple_of(core * columns, HD), columns)
    other = pl.ds(pl.multiple_of((1 - core) * columns, HD), columns)
    for out_ref, span in ((keep_ref, mine), (give_ref, other)):
        at = 0
        for ref in (own_ref, next_ref, half_ref):
            out_ref[at:at + ref.shape[0], :] = ref[:, span]
            at += ref.shape[0]


def cut_columns(places, weights):
    columns = weights[0].shape[1] // 2
    one = jax.ShapeDtypeStruct((sum(w.shape[0] for w in weights), columns), BF16)
    return pl.pallas_call(
        lambda *refs: cut_body(columns, *refs),
        out_shape=(one, one),
        in_specs=[SCALAR] + [WHOLE] * len(weights),
        out_specs=(WHOLE, WHOLE),
        compiler_params=limit(8),
        cost_estimate=pl.CostEstimate(flops=1000000, bytes_accessed=4000000, transcendentals=0),
        name="cut_columns",
    )(places, *weights)


def project_body(rows, at_ref, attn_ref, keep_ref, got_ref, others_ref, out_ref, tan_ref, left, right):
    core, half, part = at_ref[0], at_ref[1], HD // 2
    for c, ref in enumerate((keep_ref, got_ref)):
        first, theirs = 4 * c, (HD + part) * c
        for n in range(4):
            head = 2 * at_ref[2 + n] + (core if c == 0 else 1 - core)
            left[:, (first + n) * HD:(first + n + 1) * HD] = attn_ref[head]
        base = first * HD
        right[base:base + 2 * HD, :] = ref[:2 * HD, :]
        right[base + 2 * HD:base + 3 * HD, :] = others_ref[theirs:theirs + HD, :]
        low = base + 3 * HD
        right[pl.ds(pl.multiple_of(low + half * part, part), part), :] = ref[2 * HD:, :]
        right[pl.ds(pl.multiple_of(low + (1 - half) * part, part), part), :] = others_ref[theirs + HD:theirs + HD + part, :]
    total = dot_nn(left[...], right[...])
    out_ref[...] = total[:rows].astype(BF16)
    tan_ref[...] = total[rows:].astype(BF16)


def project(places, attn, keep, got, others):
    heads, both, _ = attn.shape
    columns = keep.shape[1]
    one = jax.ShapeDtypeStruct((both // 2, columns), BF16)
    return pl.pallas_call(
        lambda *refs: project_body(both // 2, *refs),
        out_shape=(one, one),
        in_specs=[SCALAR] + [WHOLE] * 4,
        out_specs=(WHOLE, WHOLE),
        scratch_shapes=[
            pltpu.VMEM((both, heads * HD), BF16),
            pltpu.VMEM((heads * HD, columns), BF16),
        ],
        compiler_params=limit(12),
        cost_estimate=pl.CostEstimate(flops=2 * both * heads * HD * columns, bytes_accessed=4000000, transcendentals=0),
        name="project",
    )(places, attn, keep, got, others)


def prepare_body(rows, copies, q_ref, k_ref, v_ref, qt_ref, kt_ref, vt_ref, spread_ref, keys_ref):
    for n, ref in enumerate((q_ref, qt_ref)):
        value = ref[...]
        for m in range(copies):
            spread_ref[m, pl.ds(n * rows, rows), :] = value
    for n, ref in enumerate((k_ref, v_ref, kt_ref, vt_ref)):
        keys_ref[pl.ds(n * rows, rows), :] = ref[...]


def prepare(arrays, copies):
    rows = arrays[0].shape[0]
    return pl.pallas_call(
        lambda *refs: prepare_body(rows, copies, *refs),
        out_shape=(
            jax.ShapeDtypeStruct((copies, 2 * rows, HD), BF16),
            jax.ShapeDtypeStruct((4 * rows, HD), BF16),
        ),
        grid=(1,),
        in_specs=[pl.BlockSpec((rows, HD), lambda i: (0, 0))] * 6,
        out_specs=(WHOLE,) * 2,
        compiler_params=limit(56),
        name="prepare",
    )(*arrays)


def turn(array, axis, count, offset):
    return lax.ppermute(array, axis, [(i, (i + offset) % count) for i in range(count)])


def per_device(queries, key_vectors, value_vectors, query_tangent, key_tangent, value_tangent, out_weight):
    rows = queries.shape[0]
    zl, yl, core = (lax.axis_index(name) for name in ("zl", "yl", "c"))
    columns = out_weight.shape[1] // 4

    arrays = (queries, key_vectors, value_vectors, query_tangent, key_tangent, value_tangent)
    q_spread, k_own = prepare(arrays, 8)
    k_far = turn(k_own, "yh", 2, 1)
    q_all = lax.all_to_all(q_spread, ("x", "zl"), 0, 0, tiled=True)
    k_first = lax.all_gather(k_own, "zh", axis=0)
    k_first, q_all, k_far = lax.optimization_barrier((k_first, q_all, k_far))
    k_second = jnp.broadcast_to(k_far[None], (4,) + k_far.shape)
    k_second = lax.all_to_all(k_second, "zh", 0, 0, tiled=True)

    def weight_of(n, first, height):
        at = (first, ((yl + n) % 4) * columns)
        return lax.dynamic_slice(out_weight, at, (height, columns))

    step = jnp.where(zl == 0, 1, 3)
    ring = [(4 * z + y, 4 * z + (y + (1, 3)[z]) % 4) for z in range(2) for y in range(4)]
    w_own = weight_of(0, 0, HD)
    w_next = lax.ppermute(weight_of(step, 0, HD), ("zl", "yl"), ring)
    w_half = turn(weight_of(2, zl * (HD // 2), HD // 2), "yl", 4, 2)

    partial = attention(q_all, (k_first, k_second), rows)
    partial, w_next, w_half = lax.optimization_barrier((partial, w_next, w_half))
    parts = lax.all_to_all(partial, ("x", "zl"), 0, 0, tiled=True)
    heads = [yl, yl - step, yl + step, yl + 2]
    places = jnp.stack([core, zl] + [head % 4 for head in heads]).astype(jnp.int32)
    keep, give = cut_columns(places, (w_own, w_next, w_half))
    got = turn(give, "c", 2, 1)
    near = [(z, (z + 1) % 8 if z % 2 else (z - 1) % 8) for z in range(8)]
    others = lax.ppermute(jnp.concatenate([keep[HD:], got[HD:]]), ("zh", "zl"), near)
    attn = lax.all_gather(merge(parts, rows), ("yl", "c"), axis=0)
    return project(places, attn, keep, got, others)


def solution(mesh):
    split = jax.sharding.Mesh(
        mesh.devices.reshape(4, 2, 2, 4, 4, 2), ("zh", "zl", "yh", "x", "yl", "c")
    )
    seq, head = ("zh", "zl", "yh", "x"), ("yl", "c")
    block = P(seq, head)
    return jax.shard_map(
        per_device,
        mesh=split,
        in_specs=(block,) * 6 + (P(head, None),),
        out_specs=(block, block),
        check_vma=False,
    )
```

```python
import jax, jax.numpy as jnp
from jax import lax
from jax.sharding import PartitionSpec as P
from jax.experimental import pallas as pl
from jax.experimental.pallas import tpu as pltpu

HD = 128
SCALE = HD ** -0.5
LOG2E = 1.4426950408889634
STAT = 16
F32 = jnp.float32
BF16 = jnp.bfloat16


def dot_nt(a, b):
    return lax.dot_general(a, b, (((1,), (1,)), ((), ())), preferred_element_type=F32)


def dot_nn(a, b):
    return jnp.dot(a, b, preferred_element_type=F32)


def three_parts(value):
    high = value.astype(BF16).astype(F32)
    rest = value - high
    mid = rest.astype(BF16).astype(F32)
    return high, mid, (rest - mid)


WHOLE = pl.BlockSpec(memory_space=pltpu.VMEM)
SCALAR = pl.BlockSpec(memory_space=pltpu.SMEM)


def limit(mib):
    return pltpu.CompilerParams(vmem_limit_bytes=mib * 1024 * 1024)


def stat_rows(stats, rows):
    lane = lax.broadcasted_iota(jnp.int32, (rows, HD), 1)
    pick_row = lax.broadcasted_iota(jnp.int32, (STAT, HD), 0)
    pick_lane = lax.broadcasted_iota(jnp.int32, (STAT, HD), 1)
    half = STAT // 2
    low = jnp.where((pick_row == pick_lane) & (pick_row < half), 1.0, 0.0).astype(BF16)
    high = jnp.where((pick_row == pick_lane + half) & (pick_lane < half), 1.0, 0.0).astype(BF16)
    table = jnp.zeros((rows, HD), F32)
    for n, stat in enumerate(stats):
        table = jnp.where(lane == n, stat, table)
    table = jnp.concatenate([table, jnp.zeros((2 * HD - rows, HD), F32)]).astype(BF16)
    return (dot_nt(low, table[:HD]) + dot_nt(high, table[HD:])).astype(BF16)


def stat_columns(block, rows, first):
    pick_row = lax.broadcasted_iota(jnp.int32, (STAT, HD), 0)

    def turned(at):
        pick = jnp.where((pick_row >= at) & (pick_row < at + 3), 1.0, 0.0).astype(BF16)
        return lax.dot_general(block, pick, (((0,), (0,)), ((), ())), preferred_element_type=F32)

    return jnp.concatenate([turned(first), turned(first + STAT // 2)[: rows - HD]])


def attention_tile(q_ref, kk, vv, span):
    scores = dot_nt(q_ref[span, HD:], kk[:, :HD])
    slope = dot_nt(q_ref[span, :], kk[...])
    top = jnp.max(scores, axis=1, keepdims=True)
    weights = jnp.exp2((scores - top) * (SCALE * LOG2E))
    total = jnp.sum(weights, axis=1, keepdims=True)
    sloped = weights * slope
    grad = jnp.sum(sloped, axis=1, keepdims=True)
    both = dot_nn(weights.astype(BF16), vv[...])
    extra = dot_nn(sloped.astype(BF16), vv[:, :HD])
    inverse = 1.0 / total
    mean = both[:, :HD] * inverse
    slope_mean = grad * (SCALE * inverse)
    tangent = (extra * SCALE + both[:, HD:]) * inverse - slope_mean * mean
    return mean, tangent, top * SCALE + jnp.log(total), slope_mean


def attention_body(rows, step_blocks, q_ref, ka_ref, kb_ref, out_ref, qq, kk, vv):
    blocks = q_ref.shape[0]
    for b in range(blocks):
        span = pl.ds(b * rows, rows)
        qq[span, :HD] = q_ref[b, rows:]
        qq[span, HD:] = q_ref[b, :rows]
    for n, k_ref in enumerate((ka_ref, kb_ref)):
        for b in range(k_ref.shape[0]):
            span = pl.ds((n * k_ref.shape[0] + b) * rows, rows)
            kk[span, :HD] = k_ref[b, :rows]
            vv[span, :HD] = k_ref[b, rows:2 * rows]
            kk[span, HD:] = k_ref[b, 2 * rows:3 * rows]
            vv[span, HD:] = k_ref[b, 3 * rows:]
    span_rows = step_blocks * rows

    def step(i, carry):
        span = pl.ds(i * span_rows, span_rows)
        mean, tangent, log, slope = attention_tile(qq, kk, vv, span)
        stats = three_parts(log) + three_parts(slope)
        for b in range(step_blocks):
            part = slice(b * rows, (b + 1) * rows)
            at = i * step_blocks + b
            out_ref[at, :rows, :] = mean[part].astype(BF16)
            out_ref[at, rows:2 * rows, :] = tangent[part].astype(BF16)
            out_ref[at, 2 * rows:, :] = stat_rows([s[part] for s in stats], rows)
        return carry

    for i in range(blocks // step_blocks):
        step(i, 0)


def attention(queries, keys, rows, step_blocks=2):
    blocks, nkeys = queries.shape[0], sum(p.shape[0] for p in keys) * rows
    work = blocks * rows * nkeys * HD
    return pl.pallas_call(
        lambda *refs: attention_body(rows, step_blocks, *refs),
        out_shape=jax.ShapeDtypeStruct((blocks, 2 * rows + STAT, HD), BF16),
        in_specs=[WHOLE] * 3,
        out_specs=WHOLE,
        scratch_shapes=[
            pltpu.VMEM((blocks * rows, 2 * HD), BF16),
            pltpu.VMEM((nkeys, 2 * HD), BF16),
            pltpu.VMEM((nkeys, 2 * HD), BF16),
        ],
        compiler_params=limit(32),
        cost_estimate=pl.CostEstimate(flops=12 * work, bytes_accessed=4000000, transcendentals=work // HD),
        name="attention",
    )(queries, *keys)


def merged(blocks, rows):
    logs = [stat_columns(block[2 * rows:, :], rows, 0) for block in blocks]
    slopes = [stat_columns(block[2 * rows:, :], rows, 3) for block in blocks]
    top = logs[0]
    for log in logs[1:]:
        top = jnp.maximum(top, log)
    shares = [jnp.exp(log - top) for log in logs]
    total = sum(shares[1:], shares[0])
    inverse = 1.0 / total
    slope_mean = sum([s * g for s, g in zip(shares[1:], slopes[1:])], shares[0] * slopes[0]) * inverse
    mean = jnp.zeros((rows, HD), F32)
    tangent = jnp.zeros((rows, HD), F32)
    for block, share, slope in zip(blocks, shares, slopes):
        one = block[:rows, :].astype(F32)
        mean += share * one
        tangent += share * (block[rows:2 * rows, :].astype(F32) + (slope - slope_mean) * one)
    return mean * inverse, tangent * inverse, top + jnp.log(total), slope_mean


def merge_body(rows, part_ref, out_ref):
    mean, tangent, _, _ = merged([part_ref[b] for b in range(part_ref.shape[0])], rows)
    out_ref[:rows, :] = mean.astype(BF16)
    out_ref[rows:, :] = tangent.astype(BF16)


def merge(parts, rows):
    return pl.pallas_call(
        lambda *refs: merge_body(rows, *refs),
        out_shape=jax.ShapeDtypeStruct((2 * rows, HD), BF16),
        in_specs=[WHOLE],
        out_specs=WHOLE,
        compiler_params=limit(12),
        name="merge",
    )(parts)


def cut_body(columns, at_ref, own_ref, next_ref, half_ref, keep_ref, give_ref):
    core = at_ref[0]
    mine = pl.ds(pl.multiple_of(core * columns, HD), columns)
    other = pl.ds(pl.multiple_of((1 - core) * columns, HD), columns)
    for out_ref, span in ((keep_ref, mine), (give_ref, other)):
        at = 0
        for ref in (own_ref, next_ref, half_ref):
            out_ref[at:at + ref.shape[0], :] = ref[:, span]
            at += ref.shape[0]


def cut_columns(places, weights):
    columns = weights[0].shape[1] // 2
    one = jax.ShapeDtypeStruct((sum(w.shape[0] for w in weights), columns), BF16)
    return pl.pallas_call(
        lambda *refs: cut_body(columns, *refs),
        out_shape=(one, one),
        in_specs=[SCALAR] + [WHOLE] * len(weights),
        out_specs=(WHOLE, WHOLE),
        compiler_params=limit(8),
        cost_estimate=pl.CostEstimate(flops=1000000, bytes_accessed=4000000, transcendentals=0),
        name="cut_columns",
    )(places, *weights)


def project_body(rows, at_ref, attn_ref, keep_ref, got_ref, others_ref, out_ref, tan_ref, left, right):
    core, half, part = at_ref[0], at_ref[1], HD // 2
    for c, ref in enumerate((keep_ref, got_ref)):
        first, theirs = 4 * c, (HD + part) * c
        for n in range(4):
            head = 2 * at_ref[2 + n] + (core if c == 0 else 1 - core)
            left[:, (first + n) * HD:(first + n + 1) * HD] = attn_ref[head]
        base = first * HD
        right[base:base + 2 * HD, :] = ref[:2 * HD, :]
        right[base + 2 * HD:base + 3 * HD, :] = others_ref[theirs:theirs + HD, :]
        low = base + 3 * HD
        right[pl.ds(pl.multiple_of(low + half * part, part), part), :] = ref[2 * HD:, :]
        right[pl.ds(pl.multiple_of(low + (1 - half) * part, part), part), :] = others_ref[theirs + HD:theirs + HD + part, :]
    total = dot_nn(left[...], right[...])
    out_ref[...] = total[:rows].astype(BF16)
    tan_ref[...] = total[rows:].astype(BF16)


def project(places, attn, keep, got, others):
    heads, both, _ = attn.shape
    columns = keep.shape[1]
    one = jax.ShapeDtypeStruct((both // 2, columns), BF16)
    return pl.pallas_call(
        lambda *refs: project_body(both // 2, *refs),
        out_shape=(one, one),
        in_specs=[SCALAR] + [WHOLE] * 4,
        out_specs=(WHOLE, WHOLE),
        scratch_shapes=[
            pltpu.VMEM((both, heads * HD), BF16),
            pltpu.VMEM((heads * HD, columns), BF16),
        ],
        compiler_params=limit(12),
        cost_estimate=pl.CostEstimate(flops=2 * both * heads * HD * columns, bytes_accessed=4000000, transcendentals=0),
        name="project",
    )(places, attn, keep, got, others)


def prepare_body(rows, copies, q_ref, k_ref, v_ref, qt_ref, kt_ref, vt_ref, spread_ref, keys_ref):
    for n, ref in enumerate((q_ref, qt_ref)):
        value = ref[...]
        for m in range(copies):
            spread_ref[m, pl.ds(n * rows, rows), :] = value
    for n, ref in enumerate((k_ref, v_ref, kt_ref, vt_ref)):
        keys_ref[pl.ds(n * rows, rows), :] = ref[...]


def prepare(arrays, copies):
    rows = arrays[0].shape[0]
    return pl.pallas_call(
        lambda *refs: prepare_body(rows, copies, *refs),
        out_shape=(
            jax.ShapeDtypeStruct((copies, 2 * rows, HD), BF16),
            jax.ShapeDtypeStruct((4 * rows, HD), BF16),
        ),
        grid=(1,),
        in_specs=[pl.BlockSpec((rows, HD), lambda i: (0, 0))] * 6,
        out_specs=(WHOLE,) * 2,
        compiler_params=limit(56),
        name="prepare",
    )(*arrays)


def turn(array, axis, count, offset):
    return lax.ppermute(array, axis, [(i, (i + offset) % count) for i in range(count)])


def per_device(queries, key_vectors, value_vectors, query_tangent, key_tangent, value_tangent, out_weight):
    rows = queries.shape[0]
    zl, yl, core = (lax.axis_index(name) for name in ("zl", "yl", "c"))
    columns = out_weight.shape[1] // 4

    arrays = (queries, key_vectors, value_vectors, query_tangent, key_tangent, value_tangent)
    q_spread, k_own = prepare(arrays, 8)
    k_far = turn(k_own, "yh", 2, 1)
    q_all = lax.all_to_all(q_spread, ("x", "zl"), 0, 0, tiled=True)
    k_first = lax.all_gather(k_own, "zh", axis=0)
    k_first, q_all, k_far = lax.optimization_barrier((k_first, q_all, k_far))
    k_second = jnp.broadcast_to(k_far[None], (4,) + k_far.shape)
    k_second = lax.all_to_all(k_second, "zh", 0, 0, tiled=True)

    def weight_of(n, first, height):
        at = (first, ((yl + n) % 4) * columns)
        return lax.dynamic_slice(out_weight, at, (height, columns))

    step = jnp.where(zl == 0, 1, 3)
    ring = [(4 * z + y, 4 * z + (y + (1, 3)[z]) % 4) for z in range(2) for y in range(4)]
    w_own = weight_of(0, 0, HD)
    w_next = lax.ppermute(weight_of(step, 0, HD), ("zl", "yl"), ring)
    w_half = turn(weight_of(2, zl * (HD // 2), HD // 2), "yl", 4, 2)

    partial = attention(q_all, (k_first, k_second), rows)
    partial, w_next, w_half = lax.optimization_barrier((partial, w_next, w_half))
    parts = lax.all_to_all(partial, ("x", "zl"), 0, 0, tiled=True)
    heads = [yl, yl - step, yl + step, yl + 2]
    heads = [head % 4 for head in heads]
    places = jnp.stack([core, zl] + [head ^ (head >> 1) for head in heads]).astype(jnp.int32)
    keep, give = cut_columns(places, (w_own, w_next, w_half))
    got = turn(give, "c", 2, 1)
    near = [(z, (z + 1) % 8 if z % 2 else (z - 1) % 8) for z in range(8)]
    others = lax.ppermute(jnp.concatenate([keep[HD:], got[HD:]]), ("zh", "zl"), near)
    folded = [2 * y + c for y in (0, 1, 3, 2) for c in range(2)]
    attn = lax.all_gather(merge(parts, rows), ("yl", "c"), axis_index_groups=[folded], axis=0)
    return project(places, attn, keep, got, others)


def solution(mesh):
    split = jax.sharding.Mesh(
        mesh.devices.reshape(4, 2, 2, 4, 4, 2), ("zh", "zl", "yh", "x", "yl", "c")
    )
    seq, head = ("zh", "zl", "yh", "x"), ("yl", "c")
    block = P(seq, head)
    return jax.shard_map(
        per_device,
        mesh=split,
        in_specs=(block,) * 6 + (P(head, None),),
        out_specs=(block, block),
        check_vma=False,
    )
```

```python
import jax, jax.numpy as jnp
from jax import lax
from jax.sharding import PartitionSpec as P
from jax.experimental import pallas as pl
from jax.experimental.pallas import tpu as pltpu

HD = 128
SCALE = HD ** -0.5
LOG2E = 1.4426950408889634
STAT = 16
F32 = jnp.float32
BF16 = jnp.bfloat16


def dot_nt(a, b):
    return lax.dot_general(a, b, (((1,), (1,)), ((), ())), preferred_element_type=F32)


def dot_nn(a, b):
    return jnp.dot(a, b, preferred_element_type=F32)


def three_parts(value):
    high = value.astype(BF16).astype(F32)
    rest = value - high
    mid = rest.astype(BF16).astype(F32)
    return high, mid, (rest - mid)


WHOLE = pl.BlockSpec(memory_space=pltpu.VMEM)
SCALAR = pl.BlockSpec(memory_space=pltpu.SMEM)


def limit(mib):
    return pltpu.CompilerParams(vmem_limit_bytes=mib * 1024 * 1024)


def stat_rows(stats, rows):
    lane = lax.broadcasted_iota(jnp.int32, (rows, HD), 1)
    pick_row = lax.broadcasted_iota(jnp.int32, (STAT, HD), 0)
    pick_lane = lax.broadcasted_iota(jnp.int32, (STAT, HD), 1)
    half = STAT // 2
    low = jnp.where((pick_row == pick_lane) & (pick_row < half), 1.0, 0.0).astype(BF16)
    high = jnp.where((pick_row == pick_lane + half) & (pick_lane < half), 1.0, 0.0).astype(BF16)
    table = jnp.zeros((rows, HD), F32)
    for n, stat in enumerate(stats):
        table = jnp.where(lane == n, stat, table)
    table = jnp.concatenate([table, jnp.zeros((2 * HD - rows, HD), F32)]).astype(BF16)
    return (dot_nt(low, table[:HD]) + dot_nt(high, table[HD:])).astype(BF16)


def stat_columns(block, rows, first):
    pick_row = lax.broadcasted_iota(jnp.int32, (STAT, HD), 0)

    def turned(at):
        pick = jnp.where((pick_row >= at) & (pick_row < at + 3), 1.0, 0.0).astype(BF16)
        return lax.dot_general(block, pick, (((0,), (0,)), ((), ())), preferred_element_type=F32)

    return jnp.concatenate([turned(first), turned(first + STAT // 2)[: rows - HD]])


def attention_tile(q_ref, kk, vv, span):
    scores = dot_nt(q_ref[span, HD:], kk[:, :HD])
    slope = dot_nt(q_ref[span, :], kk[...])
    top = jnp.max(scores, axis=1, keepdims=True)
    weights = jnp.exp2((scores - top) * (SCALE * LOG2E))
    total = jnp.sum(weights, axis=1, keepdims=True)
    sloped = weights * slope
    grad = jnp.sum(sloped, axis=1, keepdims=True)
    both = dot_nn(weights.astype(BF16), vv[...])
    extra = dot_nn(sloped.astype(BF16), vv[:, :HD])
    inverse = 1.0 / total
    mean = both[:, :HD] * inverse
    slope_mean = grad * (SCALE * inverse)
    tangent = (extra * SCALE + both[:, HD:]) * inverse - slope_mean * mean
    return mean, tangent, top * SCALE + jnp.log(total), slope_mean


def attention_body(rows, step_blocks, q_ref, ka_ref, kb_ref, out_ref, qq, kk, vv):
    blocks = q_ref.shape[0]
    for b in range(blocks):
        span = pl.ds(b * rows, rows)
        qq[span, :HD] = q_ref[b, rows:]
        qq[span, HD:] = q_ref[b, :rows]
    for n, k_ref in enumerate((ka_ref, kb_ref)):
        for b in range(k_ref.shape[0]):
            span = pl.ds((n * k_ref.shape[0] + b) * rows, rows)
            kk[span, :HD] = k_ref[b, :rows]
            vv[span, :HD] = k_ref[b, rows:2 * rows]
            kk[span, HD:] = k_ref[b, 2 * rows:3 * rows]
            vv[span, HD:] = k_ref[b, 3 * rows:]
    span_rows = step_blocks * rows

    def step(i, carry):
        span = pl.ds(i * span_rows, span_rows)
        mean, tangent, log, slope = attention_tile(qq, kk, vv, span)
        stats = three_parts(log) + three_parts(slope)
        for b in range(step_blocks):
            part = slice(b * rows, (b + 1) * rows)
            at = i * step_blocks + b
            out_ref[at, :rows, :] = mean[part].astype(BF16)
            out_ref[at, rows:2 * rows, :] = tangent[part].astype(BF16)
            out_ref[at, 2 * rows:, :] = stat_rows([s[part] for s in stats], rows)
        return carry

    for i in range(blocks // step_blocks):
        step(i, 0)


def attention(queries, keys, rows, step_blocks=2):
    blocks, nkeys = queries.shape[0], sum(p.shape[0] for p in keys) * rows
    work = blocks * rows * nkeys * HD
    return pl.pallas_call(
        lambda *refs: attention_body(rows, step_blocks, *refs),
        out_shape=jax.ShapeDtypeStruct((blocks, 2 * rows + STAT, HD), BF16),
        in_specs=[WHOLE] * 3,
        out_specs=WHOLE,
        scratch_shapes=[
            pltpu.VMEM((blocks * rows, 2 * HD), BF16),
            pltpu.VMEM((nkeys, 2 * HD), BF16),
            pltpu.VMEM((nkeys, 2 * HD), BF16),
        ],
        compiler_params=limit(32),
        cost_estimate=pl.CostEstimate(flops=12 * work, bytes_accessed=4000000, transcendentals=work // HD),
        name="attention",
    )(queries, *keys)


def merged(blocks, rows):
    logs = [stat_columns(block[2 * rows:, :], rows, 0) for block in blocks]
    slopes = [stat_columns(block[2 * rows:, :], rows, 3) for block in blocks]
    top = logs[0]
    for log in logs[1:]:
        top = jnp.maximum(top, log)
    shares = [jnp.exp(log - top) for log in logs]
    total = sum(shares[1:], shares[0])
    inverse = 1.0 / total
    slope_mean = sum([s * g for s, g in zip(shares[1:], slopes[1:])], shares[0] * slopes[0]) * inverse
    mean = jnp.zeros((rows, HD), F32)
    tangent = jnp.zeros((rows, HD), F32)
    for block, share, slope in zip(blocks, shares, slopes):
        one = block[:rows, :].astype(F32)
        mean += share * one
        tangent += share * (block[rows:2 * rows, :].astype(F32) + (slope - slope_mean) * one)
    return mean * inverse, tangent * inverse, top + jnp.log(total), slope_mean


def merge_body(rows, part_ref, out_ref):
    mean, tangent, _, _ = merged([part_ref[b] for b in range(part_ref.shape[0])], rows)
    out_ref[:rows, :] = mean.astype(BF16)
    out_ref[rows:, :] = tangent.astype(BF16)


def merge(parts, rows):
    return pl.pallas_call(
        lambda *refs: merge_body(rows, *refs),
        out_shape=jax.ShapeDtypeStruct((2 * rows, HD), BF16),
        in_specs=[WHOLE],
        out_specs=WHOLE,
        compiler_params=limit(12),
        name="merge",
    )(parts)


def cut_body(columns, at_ref, own_ref, next_ref, half_ref, keep_ref, give_ref):
    core = at_ref[0]
    mine = pl.ds(pl.multiple_of(core * columns, HD), columns)
    other = pl.ds(pl.multiple_of((1 - core) * columns, HD), columns)
    for out_ref, span in ((keep_ref, mine), (give_ref, other)):
        at = 0
        for ref in (own_ref, next_ref, half_ref):
            out_ref[at:at + ref.shape[0], :] = ref[:, span]
            at += ref.shape[0]


def cut_columns(places, weights):
    columns = weights[0].shape[1] // 2
    one = jax.ShapeDtypeStruct((sum(w.shape[0] for w in weights), columns), BF16)
    return pl.pallas_call(
        lambda *refs: cut_body(columns, *refs),
        out_shape=(one, one),
        in_specs=[SCALAR] + [WHOLE] * len(weights),
        out_specs=(WHOLE, WHOLE),
        compiler_params=limit(8),
        cost_estimate=pl.CostEstimate(flops=1000000, bytes_accessed=4000000, transcendentals=0),
        name="cut_columns",
    )(places, *weights)


def project_body(rows, at_ref, attn_ref, keep_ref, got_ref, others_ref, out_ref, tan_ref, left, right):
    core, half, part = at_ref[0], at_ref[1], HD // 2
    total = jnp.zeros((2 * rows, keep_ref.shape[1]), F32)
    for c, ref in enumerate((keep_ref, got_ref)):
        first, theirs = 4 * c, (HD + part) * c
        for n in range(4):
            head = 2 * at_ref[2 + n] + (core if c == 0 else 1 - core)
            left[:, (first + n) * HD:(first + n + 1) * HD] = attn_ref[head]
        base = 2 * HD * c
        right[base:base + HD, :] = others_ref[theirs:theirs + HD, :]
        low = base + HD
        right[pl.ds(pl.multiple_of(low + half * part, part), part), :] = ref[2 * HD:, :]
        right[pl.ds(pl.multiple_of(low + (1 - half) * part, part), part), :] = others_ref[theirs + HD:theirs + HD + part, :]
        at = first * HD
        total += dot_nn(left[:, at:at + 2 * HD], ref[:2 * HD, :])
        total += dot_nn(left[:, at + 2 * HD:at + 4 * HD], right[base:base + 2 * HD, :])
    out_ref[...] = total[:rows].astype(BF16)
    tan_ref[...] = total[rows:].astype(BF16)


def project(places, attn, keep, got, others):
    heads, both, _ = attn.shape
    columns = keep.shape[1]
    one = jax.ShapeDtypeStruct((both // 2, columns), BF16)
    return pl.pallas_call(
        lambda *refs: project_body(both // 2, *refs),
        out_shape=(one, one),
        in_specs=[SCALAR] + [WHOLE] * 4,
        out_specs=(WHOLE, WHOLE),
        scratch_shapes=[
            pltpu.VMEM((both, heads * HD), BF16),
            pltpu.VMEM((heads // 2 * HD, columns), BF16),
        ],
        compiler_params=limit(12),
        cost_estimate=pl.CostEstimate(flops=2 * both * heads * HD * columns, bytes_accessed=4000000, transcendentals=0),
        name="project",
    )(places, attn, keep, got, others)


def prepare_body(rows, copies, q_ref, k_ref, v_ref, qt_ref, kt_ref, vt_ref, spread_ref, keys_ref):
    for n, ref in enumerate((q_ref, qt_ref)):
        value = ref[...]
        for m in range(copies):
            spread_ref[m, pl.ds(n * rows, rows), :] = value
    for n, ref in enumerate((k_ref, v_ref, kt_ref, vt_ref)):
        keys_ref[pl.ds(n * rows, rows), :] = ref[...]


def prepare(arrays, copies):
    rows = arrays[0].shape[0]
    return pl.pallas_call(
        lambda *refs: prepare_body(rows, copies, *refs),
        out_shape=(
            jax.ShapeDtypeStruct((copies, 2 * rows, HD), BF16),
            jax.ShapeDtypeStruct((4 * rows, HD), BF16),
        ),
        grid=(1,),
        in_specs=[pl.BlockSpec((rows, HD), lambda i: (0, 0))] * 6,
        out_specs=(WHOLE,) * 2,
        compiler_params=limit(56),
        name="prepare",
    )(*arrays)


def turn(array, axis, count, offset):
    return lax.ppermute(array, axis, [(i, (i + offset) % count) for i in range(count)])


def per_device(queries, key_vectors, value_vectors, query_tangent, key_tangent, value_tangent, out_weight):
    rows = queries.shape[0]
    zl, yl, core = (lax.axis_index(name) for name in ("zl", "yl", "c"))
    columns = out_weight.shape[1] // 4

    arrays = (queries, key_vectors, value_vectors, query_tangent, key_tangent, value_tangent)
    q_spread, k_own = prepare(arrays, 8)
    k_far = turn(k_own, "yh", 2, 1)
    q_all = lax.all_to_all(q_spread, ("x", "zl"), 0, 0, tiled=True)
    k_first = lax.all_gather(k_own, "zh", axis=0)
    k_first, q_all, k_far = lax.optimization_barrier((k_first, q_all, k_far))
    k_second = jnp.broadcast_to(k_far[None], (4,) + k_far.shape)
    k_second = lax.all_to_all(k_second, "zh", 0, 0, tiled=True)

    def weight_of(n, first, height):
        at = (first, ((yl + n) % 4) * columns)
        return lax.dynamic_slice(out_weight, at, (height, columns))

    step = jnp.where(zl == 0, 1, 3)
    ring = [(4 * z + y, 4 * z + (y + (1, 3)[z]) % 4) for z in range(2) for y in range(4)]
    w_own = weight_of(0, 0, HD)
    w_next = lax.ppermute(weight_of(step, 0, HD), ("zl", "yl"), ring)
    w_half = turn(weight_of(2, zl * (HD // 2), HD // 2), "yl", 4, 2)

    partial = attention(q_all, (k_first, k_second), rows)
    partial, w_next, w_half = lax.optimization_barrier((partial, w_next, w_half))
    parts = lax.all_to_all(partial, ("x", "zl"), 0, 0, tiled=True)
    heads = [yl, yl - step, yl + step, yl + 2]
    heads = [head % 4 for head in heads]
    places = jnp.stack([core, zl] + [head ^ (head >> 1) for head in heads]).astype(jnp.int32)
    keep, give = cut_columns(places, (w_own, w_next, w_half))
    got = turn(give, "c", 2, 1)
    near = [(z, (z + 1) % 8 if z % 2 else (z - 1) % 8) for z in range(8)]
    others = lax.ppermute(jnp.concatenate([keep[HD:], got[HD:]]), ("zh", "zl"), near)
    folded = [2 * y + c for y in (0, 1, 3, 2) for c in range(2)]
    attn = lax.all_gather(merge(parts, rows), ("yl", "c"), axis_index_groups=[folded], axis=0)
    return project(places, attn, keep, got, others)


def solution(mesh):
    split = jax.sharding.Mesh(
        mesh.devices.reshape(4, 2, 2, 4, 4, 2), ("zh", "zl", "yh", "x", "yl", "c")
    )
    seq, head = ("zh", "zl", "yh", "x"), ("yl", "c")
    block = P(seq, head)
    return jax.shard_map(
        per_device,
        mesh=split,
        in_specs=(block,) * 6 + (P(head, None),),
        out_specs=(block, block),
        check_vma=False,
    )
```
